128 devices in a mesh: atm: 8 (over x, core), ice: 16 (over y, z).
Axes of the slice: x: 4, y: 4, z: 4, core: 2. Of those that a mesh axis runs over, the one named last changes fastest.
Arguments:
- atmospheric_driver: float32 [8, 1310720], P(None, ('atm', 'ice')), may hold values from 0 to 1
- dispatcher_own_records: int32 [8388608], P(('atm', 'ice')), may hold values from -1 to 10239, as said below
- overlay_holder_position: int32 [4, 2097152], P(None, ('atm', 'ice')), may hold values from 0 to 65535, as said below
- overlay_regrid_factor: float32 [4, 2097152], P(None, ('atm', 'ice')), may hold values from 0.05 to 0.5
- thermal_excess: float32 [30, 2097152], P(None, ('atm', 'ice')), may hold values from -1 to 0
- meltwater: float32 [30, 2097152], P(None, ('atm', 'ice')), may hold values from 0 to 0.3
- snowpack_compactness: float32 [30, 2097152], P(None, ('atm', 'ice')), may hold values from 0.3 to 0.9
- retention_limit: float32 [30, 2097152], P(None, ('atm', 'ice')), may hold values from 0.05 to 0.5
Outputs:
- class_balance: float32 [1310720], P(('atm', 'ice'))
- class_albedo: float32 [1310720], P(('atm', 'ice'))
- thermal_after_hour: float32 [30, 2097152], P(None, ('atm', 'ice'))
- meltwater_after_hour: float32 [30, 2097152], P(None, ('atm', 'ice'))
The draws below stay inside these ranges and needn't reach their ends.
Inputs may be any that keep to these rules, and one draw needn't show every extreme that they name: `dispatcher_own_records`: live entries are local rows of the sender (0 to 10239); the rest are -1, and in each (sending block, receiving block) pair the live entries come first. Write an owner's block index as atm index times the size of the ice axis plus ice index. Block b takes live slots only from four senders, each with at least one live slot: b itself, the two owners with the same atm index and ice index one lower and one higher (wrapping around), and the owner with the same ice index and atm index half the size of the atm axis further on (wrapping around); every other pair has none. `overlay_holder_position`: every intersection names a live slot: index s * 512 + slot with dispatcher_own_records[s, b, slot] not -1, b the cell's block.
All inputs are finite; a program needn't handle non-finite values.
Results may differ from the reference program's by a relative error of at most 0.0003.
Values sent between devices are 32-bit elements; how exact they have to be, the bound alone decides.
No kernel may reach another device: no remote copies, remote signals or barrier semaphores. Data moves between devices by JAX's collectives and lax.ppermute only.
A program may use at most 64 MiB of HBM per device.

```python
import math
import jax
import jax.numpy as jnp
from jax import lax

FIELDS = 8
CLASSES = 10
SNOWPACK_STRATA = 30
INTERSECTIONS = 4
DIFFUSION_ITERS = 4
PERCOLATE_ROUNDS = 6
COLS_DEV = 1024
GLACIER_PER_PART = 16384
SEND_DEV = 65536
NROWS = 1310720
GLACIER_GRIDPTS = 2097152
N_ATM = 8
N_ICE = 16


def source_owners(owner):
    atm_pos = owner // N_ICE
    ice_pos = owner % N_ICE
    return jnp.stack([owner, atm_pos * N_ICE + (ice_pos - 1) % N_ICE, atm_pos * N_ICE + (ice_pos + 1) % N_ICE, (atm_pos + N_ATM // 2) % N_ATM * N_ICE + ice_pos], axis=-1)


def live_counts(key):
    holder_partitions = N_ATM * N_ICE
    slots = SEND_DEV // holder_partitions
    key = jax.random.fold_in(key, 11)
    initial_element, second = jax.random.split(key)
    base = jax.random.randint(initial_element, (holder_partitions, holder_partitions), max(1, slots // 8), slots // 2 + 1)
    shift = jax.random.randint(second, (), 0, 4)
    busy = (jnp.arange(holder_partitions) + shift) % 4 == 0
    counts = jnp.where(busy[None, :], slots, base)
    sources = source_owners(jnp.arange(holder_partitions))
    near = jnp.any(jnp.arange(holder_partitions)[:, None, None] == sources[None, :, :], axis=-1)
    return jnp.where(near, counts, 0).astype(jnp.int32)


def draw_dispatcher_own_records(key, part):
    counts = live_counts(key)
    key = jax.random.fold_in(key, 1)
    holder_partitions = N_ATM * N_ICE
    slots = SEND_DEV // holder_partitions
    rows = jax.random.randint(key, (holder_partitions, holder_partitions, slots), 0, COLS_DEV * CLASSES)
    live = jnp.arange(slots)[None, None, :] < counts[:, :, None]
    return jnp.where(live, rows, -1).reshape(-1).astype(jnp.int32)


def draw_overlay_holder_position(key, part):
    counts = live_counts(key)
    key = jax.random.fold_in(key, 2)
    holder_partitions = N_ATM * N_ICE
    slots = SEND_DEV // holder_partitions
    initial_element, second = jax.random.split(key)
    shape = (INTERSECTIONS, holder_partitions * GLACIER_PER_PART)
    owner = jnp.broadcast_to(jnp.arange(holder_partitions * GLACIER_PER_PART) // GLACIER_PER_PART, shape)
    pick = jax.random.randint(initial_element, shape, 0, 4)
    sources = source_owners(owner)
    source = jnp.sum(jnp.where(jnp.arange(4) == pick[..., None], sources, 0), axis=-1)
    limit = counts[source, owner]
    slot = jax.random.randint(second, shape, 0, limit)
    return (source * slots + slot).astype(jnp.int32)


def level_of(own_key, dims, cuts, low, top_value):
    def one(dim, blocks):
        draws = jax.random.uniform(jax.random.fold_in(jax.random.fold_in(own_key, 6), dim), (blocks,), jnp.float32, low / len(cuts), top_value / len(cuts))
        return jnp.repeat(jnp.exp(draws), dims[dim] // blocks).reshape((-1,) + (1,) * (len(dims) - dim - 1))

    level = one(*cuts[0])
    for cut in cuts[1:]:
        level = level * one(*cut)
    return level


def setup_inputs(seed: int = 0) -> dict:
    key_list = jax.random.split(jax.random.key(seed), 9)
    atmospheric_driver = jnp.clip(1.0 * jax.random.uniform(key_list[0], (FIELDS, NROWS), jnp.float32) ** level_of(key_list[0], (FIELDS, NROWS), ((1, 128),), -0.2, 0.2), 0.0, 1.0)
    dispatcher_own_records = draw_dispatcher_own_records(jax.random.fold_in(key_list[8], 71), 0)
    overlay_holder_position = draw_overlay_holder_position(jax.random.fold_in(key_list[8], 71), 0)
    overlay_regrid_factor = jnp.clip(jnp.exp(math.log(0.5) - 2.3025851 * jax.random.uniform(key_list[3], (INTERSECTIONS, GLACIER_GRIDPTS), jnp.float32) ** level_of(key_list[3], (INTERSECTIONS, GLACIER_GRIDPTS), ((1, 128),), -0.2, 0.2)), 0.05, 0.5)
    thermal_excess = jnp.clip(-1.0 + 1.0 * jax.random.uniform(key_list[4], (SNOWPACK_STRATA, GLACIER_GRIDPTS), jnp.float32) ** level_of(key_list[4], (SNOWPACK_STRATA, GLACIER_GRIDPTS), ((1, 128),), -0.2, 0.2), -1.0, 0.0)
    meltwater = jnp.clip(0.3 * jax.random.uniform(key_list[5], (SNOWPACK_STRATA, GLACIER_GRIDPTS), jnp.float32) ** level_of(key_list[5], (SNOWPACK_STRATA, GLACIER_GRIDPTS), ((1, 128),), -0.2, 0.2), 0.0, 0.3)
    snowpack_compactness = jnp.clip(0.3 + 0.59999996 * jax.random.uniform(key_list[6], (SNOWPACK_STRATA, GLACIER_GRIDPTS), jnp.float32) ** level_of(key_list[6], (SNOWPACK_STRATA, GLACIER_GRIDPTS), ((1, 128),), -0.2, 0.2), 0.3, 0.9)
    retention_limit = jnp.clip(jnp.exp(math.log(0.5) - 2.3025851 * jax.random.uniform(key_list[7], (SNOWPACK_STRATA, GLACIER_GRIDPTS), jnp.float32) ** level_of(key_list[7], (SNOWPACK_STRATA, GLACIER_GRIDPTS), ((1, 128),), -0.2, 0.2)), 0.05, 0.5)
    return dict(atmospheric_driver=atmospheric_driver, dispatcher_own_records=dispatcher_own_records, overlay_holder_position=overlay_holder_position, overlay_regrid_factor=overlay_regrid_factor, thermal_excess=thermal_excess, meltwater=meltwater, snowpack_compactness=snowpack_compactness, retention_limit=retention_limit)


def snowpack_condition(driven_condition, thermal_excess, meltwater, snowpack_compactness, retention_limit):
    atmospheric_profile = 2.0 * driven_condition[0] - 1.0
    snow = driven_condition[3]
    rain = driven_condition[4]
    breeze_magnitude = driven_condition[6]
    skin_reflectivity = 0.45 + 0.4 * snow / (snow + 0.1) - 0.1 * jnp.maximum(atmospheric_profile, 0.0)
    thermal_transport = 1.5 * (1.0 - skin_reflectivity) * driven_condition[1] + 0.6 * (driven_condition[2] - 0.5) + 0.5 * breeze_magnitude * (atmospheric_profile - thermal_excess[0]) + 0.3 * breeze_magnitude * (driven_condition[5] - driven_condition[7])
    uppermost_stratum = thermal_excess[0] + 0.5 * thermal_transport
    thermal_excess = jnp.concatenate([jnp.minimum(uppermost_stratum, 0.0)[None], thermal_excess[1:]], axis=0)
    meltwater = jnp.concatenate([(meltwater[0] + jnp.maximum(uppermost_stratum, 0.0) + rain)[None], meltwater[1:]], axis=0)
    conductance = 0.2 + 0.25 * snowpack_compactness
    across_partitions = 0.5 * (conductance[1:] + conductance[:-1])
    nothing_scalar = jnp.zeros_like(thermal_excess[:1])
    for sweep in range(DIFFUSION_ITERS):
        meltwater_drainage = across_partitions * (thermal_excess[1:] - thermal_excess[:-1])
        thermal_excess = thermal_excess + jnp.concatenate([meltwater_drainage, nothing_scalar], axis=0) - jnp.concatenate([nothing_scalar, meltwater_drainage], axis=0)
    runoff = jnp.zeros_like(snow)
    for sweep in range(PERCOLATE_ROUNDS):
        excess = jnp.maximum(meltwater - retention_limit, 0.0)
        meltwater = meltwater - excess + jnp.concatenate([nothing_scalar, excess[:-1]], axis=0)
        runoff = runoff + excess[-1]
        solidified_melt = jnp.minimum(meltwater, 0.5 * jnp.maximum(-thermal_excess, 0.0))
        meltwater = meltwater - solidified_melt
        thermal_excess = thermal_excess + 1.5 * solidified_melt
    accumulation_budget = snow + rain - runoff - 0.2 * breeze_magnitude * (driven_condition[7] - driven_condition[5])
    return accumulation_budget, skin_reflectivity, thermal_excess, meltwater


def reference(atmospheric_driver, dispatcher_own_records, overlay_holder_position, overlay_regrid_factor, thermal_excess, meltwater, snowpack_compactness, retention_limit):
    holder_partitions = N_ATM * N_ICE
    owner_rows = COLS_DEV * CLASSES
    slots = SEND_DEV // holder_partitions
    record_number = owner_rows * holder_partitions
    routes = dispatcher_own_records.reshape(holder_partitions, holder_partitions, slots)
    starts = (jnp.arange(holder_partitions, dtype=jnp.int32) * owner_rows)[:, None]

    def partition(carry, owner):
        local = routes[:, owner, :]
        live = local >= 0
        target = jnp.where(live, starts + local, record_number).reshape(-1).astype(jnp.int32)
        picked = jnp.take(atmospheric_driver, jnp.minimum(target, record_number - 1), axis=1)
        table = jnp.where(live.reshape(-1)[None, :], picked, 0.0)
        initial_element = (owner * GLACIER_PER_PART).astype(jnp.int32)
        slot = lax.dynamic_slice_in_dim(overlay_holder_position, initial_element, GLACIER_PER_PART, 1)
        weight = lax.dynamic_slice_in_dim(overlay_regrid_factor, initial_element, GLACIER_PER_PART, 1)
        driven_condition = jnp.sum(jnp.take(table, slot, axis=1) * weight[None], axis=1)
        accumulation_budget, skin_reflectivity, temp, wet = snowpack_condition(driven_condition,
                                          lax.dynamic_slice_in_dim(thermal_excess, initial_element, GLACIER_PER_PART, 1),
                                          lax.dynamic_slice_in_dim(meltwater, initial_element, GLACIER_PER_PART, 1),
                                          lax.dynamic_slice_in_dim(snowpack_compactness, initial_element, GLACIER_PER_PART, 1),
                                          lax.dynamic_slice_in_dim(retention_limit, initial_element, GLACIER_PER_PART, 1))
        terms = jnp.stack([accumulation_budget, skin_reflectivity])[:, None, :] * weight[None]
        flat = slot.reshape(-1)
        sums = jax.vmap(lambda t: jax.ops.segment_sum(t.reshape(-1), flat, num_segments=holder_partitions * slots))(terms)
        added = jax.vmap(lambda t: jax.ops.segment_sum(t, target, num_segments=record_number + 1))(sums)
        return carry + added, (temp, wet)

    starting_guess = jnp.zeros((2, record_number + 1), jnp.float32)
    grand_aggregates, (strata_warmth, moistened) = lax.scan(partition, starting_guess, jnp.arange(holder_partitions, dtype=jnp.int32))
    thermal_after_hour = jnp.transpose(strata_warmth, (1, 0, 2)).reshape(SNOWPACK_STRATA, holder_partitions * GLACIER_PER_PART)
    meltwater_after_hour = jnp.transpose(moistened, (1, 0, 2)).reshape(SNOWPACK_STRATA, holder_partitions * GLACIER_PER_PART)
    return grand_aggregates[0, :record_number], grand_aggregates[1, :record_number], thermal_after_hour, meltwater_after_hour
```

```python
import jax
import jax.numpy as jnp
import numpy as np
from jax import lax
from jax.experimental import pallas as pl
from jax.experimental.pallas import tpu as pltpu
from jax.sharding import PartitionSpec as P

DIFFUSION_ITERS = 4
PERCOLATE_ROUNDS = 6
LANES = 128
TILE = 1024
F32 = jnp.float32
BF16 = jnp.bfloat16
VMEM_LIMIT = 48 << 20


def kernel_params():
    return pltpu.CompilerParams(vmem_limit_bytes=VMEM_LIMIT)


def spread(row):
    return jnp.broadcast_to(row, (8, LANES))


def pick_kernel(ids, records, driver, *outs):
    fields, rows = driver.shape
    for place, out in enumerate(outs):
        block = records[ids[place]]
        for j in range(block.shape[0]):
            index = spread(block[j : j + 1, :])
            low = index & (LANES - 1)
            high = index >> 7
            total = jnp.zeros((fields, LANES), F32)
            for c in range(rows // LANES):
                found = jnp.take_along_axis(
                    driver[:, c * LANES : (c + 1) * LANES], low, axis=1
                )
                total = jnp.where(high == c, found, total)
            out[:, j * LANES : (j + 1) * LANES] = total


def pick_rows(ids, records, driver, slots):
    fields = driver.shape[0]
    return pl.pallas_call(
        pick_kernel,
        out_shape=[jax.ShapeDtypeStruct((fields, slots), F32)] * 4,
        in_specs=[
            pl.BlockSpec(memory_space=pltpu.SMEM),
            pl.BlockSpec(memory_space=pltpu.VMEM),
            pl.BlockSpec(memory_space=pltpu.VMEM),
        ],
        out_specs=[pl.BlockSpec(memory_space=pltpu.VMEM)] * 4,
        compiler_params=kernel_params(),
        name="pick_rows",
    )(ids, records, driver)


def to_layers(block, scratch, column, layers):
    for i in range(0, layers, 8):
        height = min(8, layers - i)
        for j in range(8):
            scratch[pl.ds(i * 8 + j * 8, height), :] = block[
                pl.ds(i, height), pl.ds(column + j * LANES, LANES)
            ]


def layer(scratch, l):
    return scratch[pl.ds((l // 8) * 64 + l % 8, 8, stride=8), :]


def put_layer(scratch, l, value):
    scratch[pl.ds((l // 8) * 64 + l % 8, 8, stride=8), :] = value


def conduct(load_temp, load_density, first, last, layers):
    sweeps = DIFFUSION_ITERS
    low = max(first - sweeps, 0)
    high = min(last + sweeps, layers - 1)
    temps = [dict() for _ in range(sweeps + 1)]
    flows = [dict() for _ in range(sweeps + 1)]
    between = {}
    conductance = {}
    for l in range(low, high + 1):
        temps[0][l] = load_temp(l)
        conductance[l] = 0.2 + 0.25 * load_density(l)
        if l > low:
            between[l - 1] = 0.5 * (conductance[l] + conductance[l - 1])
        for s in range(1, sweeps + 1):
            step(temps, flows, between, s, l - s, low, layers)
    if high == layers - 1:
        for extra in range(1, sweeps + 1):
            for s in range(1, sweeps + 1):
                step(temps, flows, between, s, layers - 1 + extra - s, low, layers)
    return temps[sweeps]


def step(temps, flows, between, s, m, low, layers):
    before = temps[s - 1]
    if m in temps[s] or m not in before:
        return
    if m < layers - 1:
        if m + 1 not in before or m not in between:
            return
        flows[s][m] = between[m] * (before[m + 1] - before[m])
    if m > 0 and (m - 1) not in flows[s]:
        return
    value = before[m]
    if m < layers - 1:
        value = value + flows[s][m]
    if m > 0:
        value = value - flows[s][m - 1]
    temps[s][m] = value


def percolate(temp, water, limit, arriving, rounds_here):
    half = -0.5 * temp
    leaving = []
    for r in range(rounds_here):
        held = jnp.minimum(water, limit)
        leaving.append(water - held)
        if arriving is not None:
            held = held + arriving[r]
        frozen = jnp.minimum(held, jnp.maximum(half, 0.0))
        water = held - frozen
        half = half - 0.75 * frozen
    return -2.0 * half, water, leaving


def deep_start():
    return DIFFUSION_ITERS + PERCOLATE_ROUNDS


def deep_kernel(
    temp, water, density, limit, temp_out, water_out, runoff_out, surface_out, *scratch
):
    layers = temp.shape[0]
    start = deep_start()
    tiles = temp.shape[1] // TILE

    @pl.loop(0, tiles)
    def _(tile):
        column = pl.multiple_of(tile * TILE, TILE)
        st, sw, sd, sl, ot, ow = scratch
        to_layers(temp, st, column, layers)
        to_layers(water, sw, column, layers)
        to_layers(density, sd, column, layers)
        to_layers(limit, sl, column, layers)
        after = conduct(
            lambda l: layer(st, l),
            lambda l: layer(sd, l),
            DIFFUSION_ITERS + 1,
            layers - 1,
            layers,
        )
        above = DIFFUSION_ITERS
        first = layer(sw, above)
        leaving = [first - jnp.minimum(first, layer(sl, above))]
        for l in range(above + 1, layers):
            rounds = min(l - above, PERCOLATE_ROUNDS)
            t, w, gone = percolate(after[l], layer(sw, l), layer(sl, l), leaving, rounds)
            if l < start:
                gone = gone + [w - jnp.minimum(w, layer(sl, l))]
            else:
                put_layer(ot, l, t)
                put_layer(ow, l, w)
            leaving = gone[:PERCOLATE_ROUNDS]
        runoff = leaving[0]
        for r in range(1, PERCOLATE_ROUNDS):
            runoff = runoff + leaving[r]
        rows = pl.ds(pl.multiple_of(tile * 8, 8), 8)
        runoff_out[rows, :] = runoff
        surface_out[rows, :] = layer(st, 0)
        for i in range(start // 8 * 8, layers, 8):
            height = min(8, layers - i)
            for j in range(8):
                where = (pl.ds(i, height), pl.ds(column + j * LANES, LANES))
                temp_out[where] = ot[pl.ds(i * 8 + j * 8, height), :]
                water_out[where] = ow[pl.ds(i * 8 + j * 8, height), :]


def deep_layers(temp, water, density, limit):
    layers, cells = temp.shape
    width = min(cells, 2 * TILE)
    full = pl.BlockSpec((layers, width), lambda g: (0, g))
    flat = pl.BlockSpec((width // LANES, LANES), lambda g: (g, 0))
    padded = -(-layers // 8) * 64
    return pl.pallas_call(
        deep_kernel,
        grid=(cells // width,),
        out_shape=[
            jax.ShapeDtypeStruct((layers, cells), F32),
            jax.ShapeDtypeStruct((layers, cells), F32),
            jax.ShapeDtypeStruct((cells // LANES, LANES), F32),
            jax.ShapeDtypeStruct((cells // LANES, LANES), F32),
        ],
        in_specs=[full] * 4,
        out_specs=[full, full, flat, flat],
        scratch_shapes=[pltpu.VMEM((padded, LANES), F32)] * 6,
        compiler_params=kernel_params(),
        cost_estimate=pl.CostEstimate(
            flops=70 * layers * cells, bytes_accessed=24 * layers * cells, transcendentals=0
        ),
        name="deep_layers",
    )(temp, water, density, limit)


def upper_kernel(
    temp, water, density, limit, top, gain, temp_in, water_in, temp_out, water_out, *scratch
):
    rows_held = temp.shape[0]
    start = deep_start()
    tiles = temp.shape[1] // TILE

    @pl.loop(0, tiles)
    def _(tile):
        column = pl.multiple_of(tile * TILE, TILE)
        st, sw, sd, sl, ot, ow = scratch
        to_layers(temp, st, column, rows_held)
        to_layers(water, sw, column, rows_held)
        to_layers(density, sd, column, rows_held)
        to_layers(limit, sl, column, rows_held)
        rows = pl.ds(pl.multiple_of(tile * 8, 8), 8)
        top_temp = top[rows, :]
        top_gain = gain[rows, :]
        after = conduct(
            lambda l: top_temp if l == 0 else layer(st, l),
            lambda l: layer(sd, l),
            0,
            start - 1,
            1 << 20,
        )
        leaving = None
        for l in range(start):
            w = layer(sw, l)
            if l == 0:
                w = w + top_gain
            t, w, leaving = percolate(after[l], w, layer(sl, l), leaving, PERCOLATE_ROUNDS)
            put_layer(ot, l, t)
            put_layer(ow, l, w)
        for i in range(0, start, 8):
            for j in range(8):
                where = (pl.ds(i, 8), pl.ds(column + j * LANES, LANES))
                new_t = ot[pl.ds(i * 8 + j * 8, 8), :]
                new_w = ow[pl.ds(i * 8 + j * 8, 8), :]
                if i + 8 > start:
                    mine = lax.broadcasted_iota(jnp.int32, (8, LANES), 0) < start - i
                    new_t = jnp.where(mine, new_t, temp_in[where])
                    new_w = jnp.where(mine, new_w, water_in[where])
                temp_out[where] = new_t
                water_out[where] = new_w
        done = -(-start // 8) * 8
        if rows_held > done:
            where = (pl.ds(done, rows_held - done), pl.ds(column, TILE))
            temp_out[where] = temp_in[where]
            water_out[where] = water_in[where]


def upper_rows(layers):
    return -(-(deep_start() + DIFFUSION_ITERS) // 8) * 8


def upper_layers(temp, water, density, limit, top, gain, temp_deep, water_deep):
    layers, cells = temp.shape
    width = min(cells, 2 * TILE)
    rows_held = upper_rows(layers)
    part = pl.BlockSpec((rows_held, width), lambda g: (0, g))
    flat = pl.BlockSpec((width // LANES, LANES), lambda g: (g, 0))
    return pl.pallas_call(
        upper_kernel,
        grid=(cells // width,),
        out_shape=[
            jax.ShapeDtypeStruct((layers, cells), F32),
            jax.ShapeDtypeStruct((layers, cells), F32),
        ],
        in_specs=[part] * 4 + [flat] * 2 + [part] * 2,
        out_specs=[part, part],
        scratch_shapes=[pltpu.VMEM((-(-rows_held // 8) * 64, LANES), F32)] * 6,
        input_output_aliases={6: 0, 7: 1},
        compiler_params=kernel_params(),
        cost_estimate=pl.CostEstimate(
            flops=70 * rows_held * cells, bytes_accessed=24 * rows_held * cells, transcendentals=0
        ),
        name="upper_layers",
    )(temp, water, density, limit, top, gain, temp_deep, water_deep)


def two_terms(value):
    first = value.astype(BF16).astype(F32)
    return first, value - first


def cell_kernel(
    ids,
    position,
    weight,
    runoff,
    surface,
    t0,
    t1,
    t2,
    t3,
    o0,
    o1,
    o2,
    o3,
    top_out,
    gain_out,
    table,
    left,
    right,
    total,
):
    fields, slots = t0.shape
    per_place = slots // LANES
    chunks = 4 * per_place
    tiles = runoff.shape[0] // 8
    pieces = (t0, t1, t2, t3)
    for c in range(chunks):
        piece = pieces[c // per_place]
        j = c % per_place
        for f in range(fields):
            table[pl.ds((c * fields + f) * 8, 8), :] = spread(
                piece[f : f + 1, j * LANES : (j + 1) * LANES]
            )
    total[...] = jnp.zeros(total.shape, F32)
    names = [ids[c // per_place] * per_place + c % per_place for c in range(chunks)]
    names_column = jnp.zeros((chunks, LANES), jnp.int32)
    chunk_iota = lax.broadcasted_iota(jnp.int32, (chunks, LANES), 0)
    for c in range(chunks):
        names_column = jnp.where(chunk_iota == c, names[c], names_column)
    lane_iota = lax.broadcasted_iota(jnp.int32, (LANES, LANES), 0)

    @pl.loop(0, tiles)
    def _(tile):
        base = tile * 32
        rows = pl.ds(pl.multiple_of(tile * 8, 8), 8)
        forced = [jnp.zeros((8, LANES), F32) for _ in range(fields)]
        weights = []
        positions = []
        for k in range(4):
            p = position[pl.ds(base + k, 8, stride=4), :]
            wk = weight[pl.ds(base + k, 8, stride=4), :]
            positions.append(p)
            weights.append(wk)
            low = p & (LANES - 1)
            high = p >> 7
            found = [jnp.zeros((8, LANES), F32) for _ in range(fields)]
            for c in range(chunks):
                here = high == names[c]
                for f in range(fields):
                    value = jnp.take_along_axis(
                        table[pl.ds((c * fields + f) * 8, 8), :], low, axis=1
                    )
                    found[f] = jnp.where(here, value, found[f])
            for f in range(fields):
                forced[f] = forced[f] + found[f] * wk
        air = 2.0 * forced[0] - 1.0
        short, long, snow, rain, humid, wind, press = forced[1:]
        albedo = 0.45 + 0.4 * snow / (snow + 0.1) - 0.1 * jnp.maximum(air, 0.0)
        skin = surface[rows, :]
        flux = (
            1.5 * (1.0 - albedo) * short
            + 0.6 * (long - 0.5)
            + 0.5 * wind * (air - skin)
            + 0.3 * wind * (humid - press)
        )
        top = skin + 0.5 * flux
        top_out[rows, :] = jnp.minimum(top, 0.0)
        gain_out[rows, :] = jnp.maximum(top, 0.0) + rain
        balance = snow + rain - runoff[rows, :] - 0.2 * wind * (press - humid)
        for k in range(4):
            b_terms = two_terms(balance * weights[k])
            a_terms = two_terms(albedo * weights[k])
            terms = b_terms + a_terms
            for s in range(8):
                at = pl.ds((k * 8 + s) * LANES, LANES)
                p = positions[k][s : s + 1, :]
                low = jnp.broadcast_to(p & (LANES - 1), (LANES, LANES))
                right[:, at] = jnp.where(lane_iota == low, 1.0, 0.0).astype(BF16)
                here = jnp.broadcast_to(p >> 7, (chunks, LANES)) == names_column
                for n, term in enumerate(terms):
                    row = jnp.broadcast_to(term[s : s + 1, :], (chunks, LANES))
                    left[pl.ds(n * chunks, chunks), at] = jnp.where(here, row, 0.0).astype(BF16)
        total[...] += lax.dot_general(
            left[...], right[...], (((1,), (1,)), ((), ())), preferred_element_type=F32
        )

    outs = (o0, o1, o2, o3)
    for q in range(2):
        first = total[pl.ds(2 * q * chunks, chunks), :]
        second = total[pl.ds((2 * q + 1) * chunks, chunks), :]
        both = first + second
        for c in range(chunks):
            j = c % per_place
            outs[c // per_place][q : q + 1, j * LANES : (j + 1) * LANES] = both[c : c + 1, :]


def cell_sums(ids, position, weight, runoff, surface, tables):
    fields, slots = tables[0].shape
    chunks = 4 * slots // LANES
    flat = runoff.shape
    vmem = pl.BlockSpec(memory_space=pltpu.VMEM)
    return pl.pallas_call(
        cell_kernel,
        out_shape=[jax.ShapeDtypeStruct((2, slots), F32)] * 4
        + [jax.ShapeDtypeStruct(flat, F32)] * 2,
        in_specs=[pl.BlockSpec(memory_space=pltpu.SMEM)] + [vmem] * 8,
        out_specs=[vmem] * 6,
        scratch_shapes=[
            pltpu.VMEM((chunks * fields * 8, LANES), F32),
            pltpu.VMEM((4 * chunks, 4 * TILE), BF16),
            pltpu.VMEM((LANES, 4 * TILE), BF16),
            pltpu.VMEM((4 * chunks, LANES), F32),
        ],
        compiler_params=kernel_params(),
        name="cell_sums",
    )(ids, position, weight, runoff, surface, *tables)


def row_kernel(ids, records, p0, p1, p2, p3, balance_out, albedo_out, left, right):
    blocks = balance_out.shape[0]
    lane_iota = lax.broadcasted_iota(jnp.int32, (LANES, LANES), 0)
    block_iota = lax.broadcasted_iota(jnp.int32, (blocks, LANES), 0)
    for place, piece in enumerate((p0, p1, p2, p3)):
        block = records[ids[place]]
        per_place = block.shape[0]
        for j in range(per_place):
            index = block[j : j + 1, :]
            at = pl.ds((place * per_place + j) * LANES, LANES)
            low = jnp.broadcast_to(index & (LANES - 1), (LANES, LANES))
            right[:, at] = jnp.where(lane_iota == low, 1.0, 0.0).astype(BF16)
            here = jnp.broadcast_to(index >> 7, (blocks, LANES)) == block_iota
            for q in range(2):
                value = piece[q : q + 1, j * LANES : (j + 1) * LANES]
                for n, term in enumerate(two_terms(value)):
                    row = jnp.broadcast_to(term, (blocks, LANES))
                    left[pl.ds((2 * q + n) * blocks, blocks), at] = jnp.where(
                        here, row, 0.0
                    ).astype(BF16)
    total = lax.dot_general(
        left[...], right[...], (((1,), (1,)), ((), ())), preferred_element_type=F32
    )
    balance_out[...] = total[:blocks] + total[blocks : 2 * blocks]
    albedo_out[...] = total[2 * blocks : 3 * blocks] + total[3 * blocks :]


def row_sums(ids, records, pieces, rows):
    slots = pieces[0].shape[1]
    blocks = rows // LANES
    vmem = pl.BlockSpec(memory_space=pltpu.VMEM)
    return pl.pallas_call(
        row_kernel,
        out_shape=[jax.ShapeDtypeStruct((blocks, LANES), F32)] * 2,
        in_specs=[pl.BlockSpec(memory_space=pltpu.SMEM)] + [vmem] * 5,
        out_specs=[vmem] * 2,
        scratch_shapes=[
            pltpu.VMEM((4 * blocks, 4 * slots), BF16),
            pltpu.VMEM((LANES, 4 * slots), BF16),
        ],
        compiler_params=kernel_params(),
        name="row_sums",
    )(ids, records, *pieces)


def lay_flat(array):
    k, cells = array.shape
    return (
        array.reshape(k, cells // LANES, LANES).transpose(1, 0, 2).reshape(k * cells // LANES, LANES)
    )


def ring_partners(ice_count):
    even = [i ^ 1 for i in range(ice_count)]
    odd = [(((i - 1) ^ 1) + 1) % ice_count for i in range(ice_count)]
    return even, odd


def partner_table(atm_count, ice_count):
    even, odd = ring_partners(ice_count)
    table = [
        [
            a * ice_count + i,
            a * ice_count + even[i],
            a * ice_count + odd[i],
            (a + atm_count // 2) % atm_count * ice_count + i,
        ]
        for a in range(atm_count)
        for i in range(ice_count)
    ]
    return np.array(table, np.int32)


def swap_partners(pieces, atm_count, ice_count):
    even, odd = ring_partners(ice_count)
    far = [(a, (a + atm_count // 2) % atm_count) for a in range(atm_count)]
    return [
        pieces[0],
        lax.ppermute(pieces[1], "ice", list(enumerate(even))),
        lax.ppermute(pieces[2], "ice", list(enumerate(odd))),
        lax.ppermute(pieces[3], "atm", far),
    ]


def on_device(driver, records, position, weight, temp, water, density, limit):
    fields, rows = driver.shape
    atm_count = lax.axis_size("atm")
    ice_count = lax.axis_size("ice")
    owners = atm_count * ice_count
    slots = records.shape[0] // owners
    me = lax.axis_index("atm") * ice_count + lax.axis_index("ice")
    ids = jnp.asarray(partner_table(atm_count, ice_count))[me]
    records = records.reshape(owners, slots // LANES, LANES)
    picked = pick_rows(ids, records, driver, slots)
    tables = swap_partners(picked, atm_count, ice_count)
    temp_deep, water_deep, runoff, surface = deep_layers(temp, water, density, limit)
    *sums, top, gain = cell_sums(
        ids, lay_flat(position), lay_flat(weight), runoff, surface, tables
    )
    returned = swap_partners(sums, atm_count, ice_count)
    temp_new, water_new = upper_layers(
        temp, water, density, limit, top, gain, temp_deep, water_deep
    )
    balance, albedo = row_sums(ids, records, returned, rows)
    return balance.reshape(rows), albedo.reshape(rows), temp_new, water_new


def solution(mesh):
    both = ("atm", "ice")
    return jax.shard_map(
        on_device,
        mesh=mesh,
        in_specs=(P(None, both), P(both)) + (P(None, both),) * 6,
        out_specs=(P(both), P(both), P(None, both), P(None, both)),
        check_vma=False,
    )
```

```python
import functools

import jax
import jax.numpy as jnp
from jax import lax
from jax.experimental import pallas as pl
from jax.experimental.pallas import tpu as pltpu
from jax.sharding import PartitionSpec as P

DIFFUSION_ITERS = 4
PERCOLATE_ROUNDS = 6
LANES = 128
TILE = 1024
F32 = jnp.float32
BF16 = jnp.bfloat16
VMEM_SMALL = 8 << 20
VMEM_LARGE = 62 << 20
VMEM_MOST = 65280 << 10


def kernel_params(limit):
    return pltpu.CompilerParams(vmem_limit_bytes=limit)


def partner_ids(atm_count, ice_count):
    a = lax.axis_index("atm")
    i = lax.axis_index("ice")
    even = i ^ 1
    odd = lax.rem(((i + ice_count - 1) ^ 1) + 1, ice_count)
    far = lax.rem(a + atm_count // 2, atm_count)
    return (
        a * ice_count + i,
        a * ice_count + even,
        a * ice_count + odd,
        far * ice_count + i,
    )


def spread(row):
    return jnp.broadcast_to(row, (8, LANES))


def pick_kernel(mesh_shape, records, driver_any, o0, o1, o2, o3, index_out, driver, index, sems):
    ids = partner_ids(*mesh_shape)
    copies = [pltpu.make_async_copy(driver_any, driver, sems.at[4])]
    for place in range(4):
        copies.append(
            pltpu.make_async_copy(records.at[ids[place]], index.at[place], sems.at[place])
        )
    for copy in copies:
        copy.start()
    for copy in copies:
        copy.wait()
    fields, rows = driver.shape
    per_place = index.shape[1]
    for place, out in enumerate((o0, o1, o2, o3)):
        block = index[place]
        for j in range(per_place):
            row = block[j : j + 1, :]
            index_out[place * per_place + j : place * per_place + j + 1, :] = row
            where = spread(row)
            low = where & (LANES - 1)
            high = where >> 7
            total = jnp.zeros((fields, LANES), F32)
            for c in range(rows // LANES):
                found = jnp.take_along_axis(
                    driver[:, c * LANES : (c + 1) * LANES], low, axis=1
                )
                total = jnp.where(high == c, found, total)
            out[:, j * LANES : (j + 1) * LANES] = total


def pick_rows(mesh_shape, records, driver):
    fields = driver.shape[0]
    per_place = records.shape[1]
    slots = per_place * LANES
    vmem = pl.BlockSpec(memory_space=pltpu.VMEM)
    return pl.pallas_call(
        functools.partial(pick_kernel, mesh_shape),
        out_shape=[jax.ShapeDtypeStruct((fields, slots), F32)] * 4
        + [jax.ShapeDtypeStruct((4 * per_place, LANES), jnp.int32)],
        in_specs=[pl.BlockSpec(memory_space=pl.ANY)] * 2,
        out_specs=[vmem] * 5,
        scratch_shapes=[
            pltpu.VMEM(driver.shape, F32),
            pltpu.VMEM((4, per_place, LANES), jnp.int32),
            pltpu.SemaphoreType.DMA((5,)),
        ],
        compiler_params=kernel_params(VMEM_MOST),
        name="pick_rows",
    )(records, driver)


def to_layers(block, scratch, column, layers):
    for i in range(0, layers, 8):
        height = min(8, layers - i)
        for j in range(8):
            scratch[pl.ds(i * 8 + j * 8, height), :] = block[
                pl.ds(i, height), pl.ds(column + j * LANES, LANES)
            ]


def from_layers(block, scratch, column, layers):
    for i in range(0, layers, 8):
        height = min(8, layers - i)
        for j in range(8):
            block[pl.ds(i, height), pl.ds(column + j * LANES, LANES)] = scratch[
                pl.ds(i * 8 + j * 8, height), :
            ]


def layer(scratch, l):
    return scratch[pl.ds((l // 8) * 64 + l % 8, 8, stride=8), :]


def put_layer(scratch, l, value):
    scratch[pl.ds((l // 8) * 64 + l % 8, 8, stride=8), :] = value


class Conduct:
    def __init__(self, low, layers):
        self.low = low
        self.layers = layers
        self.temps = [dict() for _ in range(DIFFUSION_ITERS + 1)]
        self.flows = [dict() for _ in range(DIFFUSION_ITERS + 1)]
        self.between = {}
        self.conductance = {}

    def add(self, l, temp, density):
        self.temps[0][l] = temp
        self.conductance[l] = 0.2 + 0.25 * density
        if l > self.low:
            self.between[l - 1] = 0.5 * (self.conductance[l] + self.conductance[l - 1])
        for s in range(1, DIFFUSION_ITERS + 1):
            self.sweep(s, l - s)
        if l == self.layers - 1:
            for extra in range(1, DIFFUSION_ITERS + 1):
                for s in range(1, DIFFUSION_ITERS + 1):
                    self.sweep(s, l + extra - s)

    def sweep(self, s, m):
        before = self.temps[s - 1]
        bottom = m == self.layers - 1
        if m in self.temps[s] or m not in before:
            return
        if not bottom:
            if m + 1 not in before or m not in self.between:
                return
            self.flows[s][m] = self.between[m] * (before[m + 1] - before[m])
        if m > 0 and (m - 1) not in self.flows[s]:
            return
        value = before[m]
        if not bottom:
            value = value + self.flows[s][m]
        if m > 0:
            value = value - self.flows[s][m - 1]
        self.temps[s][m] = value


class Column:
    def __init__(self, temp, water, limit):
        self.half = -0.5 * temp
        self.water = water
        self.limit = limit
        self.leaving = {}

    def leave(self, r):
        held = jnp.minimum(self.water, self.limit)
        self.leaving[r] = self.water - held
        return held

    def round(self, r, arriving):
        held = self.leave(r)
        if arriving is not None:
            held = held + arriving
        frozen = jnp.minimum(held, jnp.maximum(self.half, 0.0))
        self.water = held - frozen
        self.half = self.half - 0.75 * frozen


def deep_steps(st, sw, sd, sl, ot, ow, layers, found):
    reach = DIFFUSION_ITERS
    conduct = Conduct(1, layers)
    columns = {}
    ready = reach
    for l in range(1, layers):
        conduct.add(l, layer(st, l), layer(sd, l))
        yield
        while ready < layers and (ready == reach or ready in conduct.temps[reach]):
            m = ready
            ready += 1
            if m == reach:
                columns[m] = Column(jnp.zeros((8, LANES), F32), layer(sw, m), layer(sl, m))
                columns[m].leave(0)
                continue
            column = Column(conduct.temps[reach][m], layer(sw, m), layer(sl, m))
            columns[m] = column
            rounds = min(m - reach, PERCOLATE_ROUNDS)
            for r in range(rounds):
                column.round(r, columns[m - 1].leaving[r])
                yield
            if rounds < PERCOLATE_ROUNDS:
                column.leave(rounds)
            else:
                put_layer(ot, m, -2.0 * column.half)
                put_layer(ow, m, column.water)
            if m - 1 >= reach + PERCOLATE_ROUNDS:
                del columns[m - 1]
            yield
    last = columns[layers - 1].leaving
    runoff = last[0]
    for r in range(1, PERCOLATE_ROUNDS):
        runoff = runoff + last[r]
    found["runoff"] = runoff
    found["columns"] = columns


def upper_steps(st, sw, sd, sl, ot, ow, top, gain, columns):
    reach = DIFFUSION_ITERS
    conduct = Conduct(0, 1 << 20)
    above = None
    for l in range(2 * reach + 1):
        conduct.add(l, top if l == 0 else layer(st, l), layer(sd, l))
        yield
        m = l - reach
        if m < 0:
            continue
        water = layer(sw, m)
        if m == 0:
            water = water + gain
        column = Column(conduct.temps[reach][m], water, layer(sl, m))
        for r in range(PERCOLATE_ROUNDS):
            column.round(r, None if above is None else above.leaving[r])
            yield
        put_layer(ot, m, -2.0 * column.half)
        put_layer(ow, m, column.water)
        above = column
    for m in range(reach + 1, reach + PERCOLATE_ROUNDS):
        column = columns[m]
        for r in range(m - reach, PERCOLATE_ROUNDS):
            column.round(r, above.leaving[r])
            yield
        put_layer(ot, m, -2.0 * column.half)
        put_layer(ow, m, column.water)
        above = column


def together(main, beside, each):
    going = True
    for _ in main:
        for _ in range(each):
            if going:
                going = next(beside, False) is None
    for _ in beside:
        pass


def two_terms(value):
    first = value.astype(BF16).astype(F32)
    return first, value - first


def gather_steps(table, low, high, weights, fields, chunks, forced):
    for k in range(len(low)):
        found = [jnp.zeros((8, LANES), F32) for _ in range(fields)]
        for c in range(chunks):
            here = high[k] == c
            for f in range(fields):
                value = jnp.take_along_axis(
                    table[pl.ds((c * fields + f) * 8, 8), :], low[k], axis=1
                )
                found[f] = jnp.where(here, value, found[f])
            yield
        for f in range(fields):
            part = found[f] * weights[k]
            forced[f] = part if k == 0 else forced[f] + part


def packed(row):
    return jnp.broadcast_to(row, (16, LANES)).astype(BF16)


def sixteens(count):
    base = lax.broadcasted_iota(jnp.int32, (16, LANES), 0)
    return [(base + 16 * j).astype(F32).astype(BF16) for j in range(count // 16)]


def scatter_steps(total, low, high, weights, values, chunks):
    one = jnp.ones((16, LANES), BF16)
    zero = jnp.zeros((16, LANES), BF16)
    lane_numbers = sixteens(LANES)
    chunk_numbers = sixteens(chunks)
    for k in range(len(low)):
        terms = [t for v in values for t in two_terms(v * weights[k])]
        low_f = low[k].astype(F32)
        high_f = high[k].astype(F32)
        lefts = []
        rights = []
        for s in range(8):
            low_row = packed(low_f[s : s + 1, :])
            high_row = packed(high_f[s : s + 1, :])
            rights.append(
                jnp.concatenate([jnp.where(low_row == n, one, zero) for n in lane_numbers], 0)
            )
            here = [high_row == n for n in chunk_numbers]
            parts = []
            for term in terms:
                row = packed(term[s : s + 1, :])
                parts += [jnp.where(h, row, zero) for h in here]
            lefts.append(jnp.concatenate(parts, 0))
            yield
        total[...] += lax.dot_general(
            jnp.concatenate(rights, 1),
            jnp.concatenate(lefts, 1),
            (((1,), (1,)), ((), ())),
            preferred_element_type=F32,
        )


def cell_kernel(mesh_shape, *refs):
    position, weight, temp, water, density, limit, t0, t1, t2, t3 = refs[:10]
    o0, o1, o2, o3, temp_out, water_out = refs[10:16]
    table, total, st, sw, sd, sl, ot, ow = refs[16:]
    fields, slots = t0.shape
    per_place = slots // LANES
    chunks = 4 * per_place
    layers, width = temp.shape
    ids = partner_ids(*mesh_shape)

    @pl.when(pl.program_id(0) == 0)
    def _():
        for c in range(chunks):
            piece = (t0, t1, t2, t3)[c // per_place]
            j = c % per_place
            for f in range(fields):
                table[pl.ds((c * fields + f) * 8, 8), :] = spread(
                    piece[f : f + 1, j * LANES : (j + 1) * LANES]
                )
        total[...] = jnp.zeros(total.shape, F32)

    @pl.loop(0, width // TILE)
    def _(tile):
        column = pl.multiple_of(tile * TILE, TILE)
        low = []
        high = []
        weights = []
        for k in range(4):
            rows = pl.ds(tile * 32 + k, 8, stride=4)
            p = position[rows, :]
            owner = p >> (slots.bit_length() - 1)
            place = jnp.zeros((8, LANES), jnp.int32)
            for n in range(1, 4):
                place = jnp.where(owner == ids[n], n, place)
            low.append(p & (LANES - 1))
            high.append(place * per_place + ((p & (slots - 1)) >> 7))
            weights.append(weight[rows, :])
        to_layers(temp, st, column, layers)
        to_layers(density, sd, column, layers)
        to_layers(water, sw, column, layers)
        to_layers(limit, sl, column, layers)
        forced = [None] * fields
        firn = {}
        together(
            gather_steps(table, low, high, weights, fields, chunks, forced),
            deep_steps(st, sw, sd, sl, ot, ow, layers, firn),
            4,
        )
        air = 2.0 * forced[0] - 1.0
        short, long, snow, rain, humid, wind, press = forced[1:]
        albedo = 0.45 + 0.4 * snow / (snow + 0.1) - 0.1 * jnp.maximum(air, 0.0)
        skin = layer(st, 0)
        flux = (
            1.5 * (1.0 - albedo) * short
            + 0.6 * (long - 0.5)
            + 0.5 * wind * (air - skin)
            + 0.3 * wind * (humid - press)
        )
        top = skin + 0.5 * flux
        balance = snow + rain - firn["runoff"] - 0.2 * wind * (press - humid)
        together(
            scatter_steps(total, low, high, weights, (balance, albedo), chunks),
            upper_steps(
                st,
                sw,
                sd,
                sl,
                ot,
                ow,
                jnp.minimum(top, 0.0),
                jnp.maximum(top, 0.0) + rain,
                firn["columns"],
            ),
            3,
        )
        from_layers(temp_out, ot, column, layers)
        from_layers(water_out, ow, column, layers)

    @pl.when(pl.program_id(0) == pl.num_programs(0) - 1)
    def _():
        sums = total[...].T
        for q in range(2):
            first = sums[2 * q * chunks : (2 * q + 1) * chunks]
            second = sums[(2 * q + 1) * chunks : (2 * q + 2) * chunks]
            both = first + second
            for c in range(chunks):
                j = c % per_place
                (o0, o1, o2, o3)[c // per_place][q : q + 1, j * LANES : (j + 1) * LANES] = both[
                    c : c + 1, :
                ]


def cell_sums(mesh_shape, position, weight, temp, water, density, limit, tables):
    fields, slots = tables[0].shape
    chunks = 4 * slots // LANES
    layers, cells = temp.shape
    width = min(cells, 2 * TILE)
    firn = pl.BlockSpec((layers, width), lambda g: (0, g))
    flat = pl.BlockSpec((4 * width // LANES, LANES), lambda g: (g, 0))
    table = pl.BlockSpec((fields, slots), lambda g: (0, 0))
    sums = pl.BlockSpec((2, slots), lambda g: (0, 0))
    padded = -(-layers // 8) * 64
    return pl.pallas_call(
        functools.partial(cell_kernel, mesh_shape),
        grid=(cells // width,),
        out_shape=[jax.ShapeDtypeStruct((2, slots), F32)] * 4
        + [jax.ShapeDtypeStruct((layers, cells), F32)] * 2,
        in_specs=[flat] * 2 + [firn] * 4 + [table] * 4,
        out_specs=[sums] * 4 + [firn] * 2,
        scratch_shapes=[
            pltpu.VMEM((chunks * fields * 8, LANES), F32),
            pltpu.VMEM((LANES, 4 * chunks), F32),
        ]
        + [pltpu.VMEM((padded, LANES), F32)] * 6,
        compiler_params=kernel_params(VMEM_LARGE),
        name="cell_sums",
    )(position, weight, temp, water, density, limit, *tables)


def row_kernel(index, p0, p1, p2, p3, balance_out, albedo_out):
    blocks = balance_out.shape[0]
    per_place = index.shape[0] // 4
    one = jnp.ones((16, LANES), BF16)
    zero = jnp.zeros((16, LANES), BF16)
    lane_numbers = sixteens(LANES)
    block_numbers = sixteens(blocks)
    rights = []
    lefts = []
    for place, piece in enumerate((p0, p1, p2, p3)):
        for j in range(per_place):
            n = place * per_place + j
            row = index[n : n + 1, :]
            low_row = packed((row & (LANES - 1)).astype(F32))
            high_row = packed((row >> 7).astype(F32))
            rights.append(
                jnp.concatenate([jnp.where(low_row == m, one, zero) for m in lane_numbers], 0)
            )
            here = [high_row == m for m in block_numbers]
            parts = []
            for q in range(2):
                for term in two_terms(piece[q : q + 1, j * LANES : (j + 1) * LANES]):
                    value = packed(term)
                    parts += [jnp.where(h, value, zero) for h in here]
            lefts.append(jnp.concatenate(parts, 0))
    total = lax.dot_general(
        jnp.concatenate(lefts, 1),
        jnp.concatenate(rights, 1),
        (((1,), (1,)), ((), ())),
        preferred_element_type=F32,
    )
    balance_out[...] = total[:blocks] + total[blocks : 2 * blocks]
    albedo_out[...] = total[2 * blocks : 3 * blocks] + total[3 * blocks :]


def row_sums(index, pieces, rows):
    blocks = rows // LANES
    vmem = pl.BlockSpec(memory_space=pltpu.VMEM)
    return pl.pallas_call(
        row_kernel,
        out_shape=[jax.ShapeDtypeStruct((blocks, LANES), F32)] * 2,
        in_specs=[vmem] * 5,
        out_specs=[vmem] * 2,
        compiler_params=kernel_params(VMEM_SMALL),
        name="row_sums",
    )(index, *pieces)


def lay_flat(array):
    k, cells = array.shape
    return (
        array.reshape(k, cells // LANES, LANES).transpose(1, 0, 2).reshape(k * cells // LANES, LANES)
    )


def ring_partners(ice_count):
    even = [i ^ 1 for i in range(ice_count)]
    odd = [(((i - 1) ^ 1) + 1) % ice_count for i in range(ice_count)]
    return even, odd


def swap_partners(pieces, atm_count, ice_count):
    even, odd = ring_partners(ice_count)
    far = [(a, (a + atm_count // 2) % atm_count) for a in range(atm_count)]
    return [
        pieces[0],
        lax.ppermute(pieces[1], "ice", list(enumerate(even))),
        lax.ppermute(pieces[2], "ice", list(enumerate(odd))),
        lax.ppermute(pieces[3], "atm", far),
    ]


def on_device(driver, records, position, weight, temp, water, density, limit):
    fields, rows = driver.shape
    atm_count = lax.axis_size("atm")
    ice_count = lax.axis_size("ice")
    mesh_shape = (atm_count, ice_count)
    owners = atm_count * ice_count
    slots = records.shape[0] // owners
    records = records.reshape(owners, slots // LANES, LANES)
    *picked, index = pick_rows(mesh_shape, records, driver)
    tables = swap_partners(picked, atm_count, ice_count)
    *sums, temp_new, water_new = cell_sums(
        mesh_shape, lay_flat(position), lay_flat(weight), temp, water, density, limit, tables
    )
    returned = swap_partners(sums, atm_count, ice_count)
    balance, albedo = row_sums(index, returned, rows)
    return balance.reshape(rows), albedo.reshape(rows), temp_new, water_new


def solution(mesh):
    both = ("atm", "ice")
    return jax.shard_map(
        on_device,
        mesh=mesh,
        in_specs=(P(None, both), P(both)) + (P(None, both),) * 6,
        out_specs=(P(both), P(both), P(None, both), P(None, both)),
        check_vma=False,
    )
```

```python
import functools

import jax
import jax.numpy as jnp
from jax import lax
from jax.experimental import pallas as pl
from jax.experimental.pallas import tpu as pltpu
from jax.sharding import PartitionSpec as P

DIFFUSION_ITERS = 4
PERCOLATE_ROUNDS = 6
LANES = 128
TILE = 1024
F32 = jnp.float32
BF16 = jnp.bfloat16
WORDS = 5
FIXED = (1 << 20) - 1
TILES = 4
VMEM_SMALL = 8 << 20
VMEM_LARGE = 62 << 20
VMEM_MOST = 65280 << 10


def kernel_params(limit):
    return pltpu.CompilerParams(vmem_limit_bytes=limit)


def partner_ids(atm_count, ice_count):
    a = lax.axis_index("atm")
    i = lax.axis_index("ice")
    even = i ^ 1
    odd = lax.rem(((i + ice_count - 1) ^ 1) + 1, ice_count)
    far = lax.rem(a + atm_count // 2, atm_count)
    return (
        a * ice_count + i,
        a * ice_count + even,
        a * ice_count + odd,
        far * ice_count + i,
    )


def spread(row):
    return jnp.broadcast_to(row, (8, LANES))


def pick_kernel(mesh_shape, records, driver_any, o0, o1, o2, o3, index_out, driver, index, sems):
    ids = partner_ids(*mesh_shape)
    copies = [pltpu.make_async_copy(driver_any, driver, sems.at[4])]
    for place in range(4):
        copies.append(
            pltpu.make_async_copy(records.at[ids[place]], index.at[place], sems.at[place])
        )
    for copy in copies:
        copy.start()
    for copy in copies:
        copy.wait()
    fields, rows = driver.shape
    per_place = index.shape[1]
    for place, out in enumerate((o0, o1, o2, o3)):
        block = index[place]
        for j in range(per_place):
            row = block[j : j + 1, :]
            index_out[place * per_place + j : place * per_place + j + 1, :] = row
            where = spread(row)
            low = where & (LANES - 1)
            high = where >> 7
            total = jnp.zeros((fields, LANES), F32)
            for c in range(rows // LANES):
                found = jnp.take_along_axis(
                    driver[:, c * LANES : (c + 1) * LANES], low, axis=1
                )
                total = jnp.where(high == c, found, total)
            out[:, j * LANES : (j + 1) * LANES] = total


def pick_rows(mesh_shape, records, driver):
    fields = driver.shape[0]
    per_place = records.shape[1]
    slots = per_place * LANES
    vmem = pl.BlockSpec(memory_space=pltpu.VMEM)
    return pl.pallas_call(
        functools.partial(pick_kernel, mesh_shape),
        out_shape=[jax.ShapeDtypeStruct((fields, slots), F32)] * 4
        + [jax.ShapeDtypeStruct((4 * per_place, LANES), jnp.int32)],
        in_specs=[pl.BlockSpec(memory_space=pl.ANY)] * 2,
        out_specs=[vmem] * 5,
        scratch_shapes=[
            pltpu.VMEM(driver.shape, F32),
            pltpu.VMEM((4, per_place, LANES), jnp.int32),
            pltpu.SemaphoreType.DMA((5,)),
        ],
        compiler_params=kernel_params(VMEM_MOST),
        name="pick_rows",
    )(records, driver)


def to_layers(block, scratch, column, layers):
    for i in range(0, layers, 8):
        height = min(8, layers - i)
        for j in range(8):
            scratch[pl.ds(i * 8 + j * 8, height), :] = block[
                pl.ds(i, height), pl.ds(column + j * LANES, LANES)
            ]


def from_layers(block, scratch, column, layers):
    for i in range(0, layers, 8):
        height = min(8, layers - i)
        for j in range(8):
            block[pl.ds(i, height), pl.ds(column + j * LANES, LANES)] = scratch[
                pl.ds(i * 8 + j * 8, height), :
            ]


def layer(scratch, l):
    return scratch[pl.ds((l // 8) * 64 + l % 8, 8, stride=8), :]


def put_layer(scratch, l, value):
    scratch[pl.ds((l // 8) * 64 + l % 8, 8, stride=8), :] = value


class Conduct:
    def __init__(self, low, layers):
        self.low = low
        self.layers = layers
        self.temps = [dict() for _ in range(DIFFUSION_ITERS + 1)]
        self.flows = [dict() for _ in range(DIFFUSION_ITERS + 1)]
        self.between = {}
        self.conductance = {}

    def add(self, l, temp, density):
        self.temps[0][l] = temp
        self.conductance[l] = 0.2 + 0.25 * density
        if l > self.low:
            self.between[l - 1] = 0.5 * (self.conductance[l] + self.conductance[l - 1])
        for s in range(1, DIFFUSION_ITERS + 1):
            self.sweep(s, l - s)
        if l == self.layers - 1:
            for extra in range(1, DIFFUSION_ITERS + 1):
                for s in range(1, DIFFUSION_ITERS + 1):
                    self.sweep(s, l + extra - s)

    def sweep(self, s, m):
        before = self.temps[s - 1]
        bottom = m == self.layers - 1
        if m in self.temps[s] or m not in before:
            return
        if not bottom:
            if m + 1 not in before or m not in self.between:
                return
            self.flows[s][m] = self.between[m] * (before[m + 1] - before[m])
        if m > 0 and (m - 1) not in self.flows[s]:
            return
        value = before[m]
        if not bottom:
            value = value + self.flows[s][m]
        if m > 0:
            value = value - self.flows[s][m - 1]
        self.temps[s][m] = value


class Column:
    def __init__(self, temp, water, limit):
        self.half = -0.5 * temp
        self.water = water
        self.limit = limit
        self.leaving = {}

    def leave(self, r):
        held = jnp.minimum(self.water, self.limit)
        self.leaving[r] = self.water - held
        return held

    def round(self, r, arriving):
        held = self.leave(r)
        if arriving is not None:
            held = held + arriving
        frozen = jnp.minimum(held, jnp.maximum(self.half, 0.0))
        self.water = held - frozen
        self.half = self.half - 0.75 * frozen


def deep_steps(st, sw, sd, sl, ot, ow, layers, found):
    reach = DIFFUSION_ITERS
    conduct = Conduct(1, layers)
    columns = {}
    ready = reach
    for l in range(1, layers):
        conduct.add(l, layer(st, l), layer(sd, l))
        yield
        while ready < layers and (ready == reach or ready in conduct.temps[reach]):
            m = ready
            ready += 1
            if m == reach:
                columns[m] = Column(jnp.zeros((8, LANES), F32), layer(sw, m), layer(sl, m))
                columns[m].leave(0)
                continue
            column = Column(conduct.temps[reach][m], layer(sw, m), layer(sl, m))
            columns[m] = column
            rounds = min(m - reach, PERCOLATE_ROUNDS)
            for r in range(rounds):
                column.round(r, columns[m - 1].leaving[r])
                yield
            if rounds < PERCOLATE_ROUNDS:
                column.leave(rounds)
            else:
                put_layer(ot, m, -2.0 * column.half)
                put_layer(ow, m, column.water)
            if m - 1 >= reach + PERCOLATE_ROUNDS:
                del columns[m - 1]
            yield
    last = columns[layers - 1].leaving
    runoff = last[0]
    for r in range(1, PERCOLATE_ROUNDS):
        runoff = runoff + last[r]
    found["runoff"] = runoff
    found["columns"] = columns


def upper_steps(st, sw, sd, sl, ot, ow, top, gain, columns):
    reach = DIFFUSION_ITERS
    conduct = Conduct(0, 1 << 20)
    above = None
    for l in range(2 * reach + 1):
        conduct.add(l, top if l == 0 else layer(st, l), layer(sd, l))
        yield
        m = l - reach
        if m < 0:
            continue
        water = layer(sw, m)
        if m == 0:
            water = water + gain
        column = Column(conduct.temps[reach][m], water, layer(sl, m))
        for r in range(PERCOLATE_ROUNDS):
            column.round(r, None if above is None else above.leaving[r])
            yield
        put_layer(ot, m, -2.0 * column.half)
        put_layer(ow, m, column.water)
        above = column
    for m in range(reach + 1, reach + PERCOLATE_ROUNDS):
        column = columns[m]
        for r in range(m - reach, PERCOLATE_ROUNDS):
            column.round(r, above.leaving[r])
            yield
        put_layer(ot, m, -2.0 * column.half)
        put_layer(ow, m, column.water)
        above = column


def together(*lines):
    ticks = 64
    for tick in range(1, ticks + 1):
        for steps, length in lines:
            for _ in range(length * tick // ticks - length * (tick - 1) // ticks):
                next(steps, None)
    for steps, _ in lines:
        for _ in steps:
            pass


def two_terms(value):
    first = value.astype(BF16).astype(F32)
    return first, value - first


def make_words(rows, scale):
    q = (rows * scale + 0.5).astype(jnp.int32)
    q = [spread(q[f : f + 1, :]) for f in range(8)]
    return [
        q[0] | ((q[5] & 0xFFF) << 20),
        q[1] | ((q[5] >> 12) << 20) | ((q[6] & 0xF) << 28),
        q[2] | (((q[6] >> 4) & 0xFFF) << 20),
        q[3] | ((q[6] >> 16) << 20) | ((q[7] & 0xFF) << 24),
        q[4] | ((q[7] >> 8) << 20),
    ]


def from_words(words):
    def high(word, bits):
        return lax.shift_right_logical(word, jnp.full(word.shape, bits, jnp.int32))

    q = [word & FIXED for word in words]
    q.append(high(words[0], 20) | ((high(words[1], 20) & 0xFF) << 12))
    q.append(
        high(words[1], 28) | (high(words[2], 20) << 4) | ((high(words[3], 20) & 0xF) << 16)
    )
    q.append(high(words[3], 24) | (high(words[4], 20) << 8))
    return [value.astype(F32) for value in q]


def gather_steps(table, low, high, weights, chunks, forced):
    for k in range(len(low)):
        found = [jnp.zeros((8, LANES), jnp.int32) for _ in range(WORDS)]
        for c in range(chunks):
            here = high[k] == c
            for n in range(WORDS):
                value = jnp.take_along_axis(
                    table[pl.ds((c * WORDS + n) * 8, 8), :], low[k], axis=1
                )
                found[n] = jnp.where(here, value, found[n])
            yield
        for f, value in enumerate(from_words(found)):
            part = value * weights[k]
            forced[f] = part if k == 0 else forced[f] + part


def packed(row):
    return jnp.broadcast_to(row, (16, LANES)).astype(BF16)


def sixteens(count):
    base = lax.broadcasted_iota(jnp.int32, (16, LANES), 0)
    return [(base + 16 * j).astype(F32).astype(BF16) for j in range(count // 16)]


def scatter_steps(total, low, high, weights, values, chunks):
    one = jnp.ones((16, LANES), BF16)
    zero = jnp.zeros((16, LANES), BF16)
    lane_numbers = sixteens(LANES)
    chunk_numbers = sixteens(chunks)
    for k in range(len(low)):
        terms = [t for v in values for t in two_terms(v * weights[k])]
        low_f = low[k].astype(F32)
        high_f = high[k].astype(F32)
        lefts = []
        rights = []
        for s in range(8):
            low_row = packed(low_f[s : s + 1, :])
            high_row = packed(high_f[s : s + 1, :])
            rights.append(
                jnp.concatenate([jnp.where(low_row == n, one, zero) for n in lane_numbers], 0)
            )
            here = [high_row == n for n in chunk_numbers]
            parts = []
            for term in terms:
                row = packed(term[s : s + 1, :])
                parts += [jnp.where(h, row, zero) for h in here]
            lefts.append(jnp.concatenate(parts, 0))
            yield
        total[...] += lax.dot_general(
            jnp.concatenate(rights, 1),
            jnp.concatenate(lefts, 1),
            (((1,), (1,)), ((), ())),
            preferred_element_type=F32,
        )


def cell_kernel(mesh_shape, *refs):
    position, weight, temp, water, density, limit, t0, t1, t2, t3 = refs[:10]
    o0, o1, o2, o3, temp_out, water_out = refs[10:16]
    table, units, total = refs[16:19]
    laid = (refs[19:25], refs[25:31])
    fields, slots = t0.shape
    per_place = slots // LANES
    chunks = 4 * per_place
    layers, width = temp.shape
    ids = partner_ids(*mesh_shape)

    @pl.when(pl.program_id(0) == 0)
    def _():
        rows = [
            (t0, t1, t2, t3)[c // per_place][
                :, (c % per_place) * LANES : (c % per_place + 1) * LANES
            ]
            for c in range(chunks)
        ]
        most = rows[0]
        for row in rows[1:]:
            most = jnp.maximum(most, row)
        most = jnp.broadcast_to(jnp.max(most, axis=1, keepdims=True), (fields, LANES))
        most = jnp.maximum(most, 1e-30)
        scale = float(FIXED) / most
        for f in range(fields):
            units[pl.ds(f * 8, 8), :] = spread(most[f : f + 1, :] * (1.0 / FIXED))
        for c in range(chunks):
            for n, word in enumerate(make_words(rows[c], scale)):
                table[pl.ds((c * WORDS + n) * 8, 8), :] = word
        total[...] = jnp.zeros(total.shape, F32)

    def load(tile):
        st, sw, sd, sl, ot, ow = laid[tile % 2]
        column = tile * TILE
        low = []
        high = []
        weights = []
        for k in range(4):
            rows = pl.ds(tile * 32 + k, 8, stride=4)
            p = position[rows, :]
            owner = p >> (slots.bit_length() - 1)
            place = jnp.zeros((8, LANES), jnp.int32)
            for n in range(1, 4):
                place = jnp.where(owner == ids[n], n, place)
            low.append(p & (LANES - 1))
            high.append(place * per_place + ((p & (slots - 1)) >> 7))
            weights.append(weight[rows, :])
        to_layers(temp, st, column, layers)
        to_layers(density, sd, column, layers)
        to_layers(water, sw, column, layers)
        to_layers(limit, sl, column, layers)
        state = {"low": low, "high": high, "weights": weights, "forced": [None] * fields}
        first = [
            (gather_steps(table, low, high, weights, chunks, state["forced"]), 64),
            (deep_steps(*laid[tile % 2], layers, state), 230),
        ]
        return state, first

    def surface(tile, state):
        forced = [value * units[pl.ds(f * 8, 8), :] for f, value in enumerate(state["forced"])]
        air = 2.0 * forced[0] - 1.0
        short, long, snow, rain, humid, wind, press = forced[1:]
        albedo = 0.45 + 0.4 * snow / (snow + 0.1) - 0.1 * jnp.maximum(air, 0.0)
        skin = layer(laid[tile % 2][0], 0)
        flux = (
            1.5 * (1.0 - albedo) * short
            + 0.6 * (long - 0.5)
            + 0.5 * wind * (air - skin)
            + 0.3 * wind * (humid - press)
        )
        top = skin + 0.5 * flux
        balance = snow + rain - state["runoff"] - 0.2 * wind * (press - humid)
        return [
            (
                scatter_steps(
                    total, state["low"], state["high"], state["weights"], (balance, albedo), chunks
                ),
                32,
            ),
            (
                upper_steps(
                    *laid[tile % 2],
                    jnp.minimum(top, 0.0),
                    jnp.maximum(top, 0.0) + rain,
                    state["columns"],
                ),
                54,
            ),
        ]

    tiles = width // TILE
    state, first = load(0)
    together(*first)
    for tile in range(tiles):
        lines = surface(tile, state)
        if tile + 1 < tiles:
            state, first = load(tile + 1)
            lines += first
        together(*lines)
        ot, ow = laid[tile % 2][4:]
        from_layers(temp_out, ot, tile * TILE, layers)
        from_layers(water_out, ow, tile * TILE, layers)

    @pl.when(pl.program_id(0) == pl.num_programs(0) - 1)
    def _():
        sums = total[...].T
        for q in range(2):
            first = sums[2 * q * chunks : (2 * q + 1) * chunks]
            second = sums[(2 * q + 1) * chunks : (2 * q + 2) * chunks]
            both = first + second
            for c in range(chunks):
                j = c % per_place
                (o0, o1, o2, o3)[c // per_place][q : q + 1, j * LANES : (j + 1) * LANES] = both[
                    c : c + 1, :
                ]


def cell_sums(mesh_shape, position, weight, temp, water, density, limit, tables):
    fields, slots = tables[0].shape
    chunks = 4 * slots // LANES
    layers, cells = temp.shape
    width = min(cells, TILES * TILE)
    firn = pl.BlockSpec((layers, width), lambda g: (0, g))
    flat = pl.BlockSpec((4 * width // LANES, LANES), lambda g: (g, 0))
    table = pl.BlockSpec((fields, slots), lambda g: (0, 0))
    sums = pl.BlockSpec((2, slots), lambda g: (0, 0))
    padded = -(-layers // 8) * 64
    return pl.pallas_call(
        functools.partial(cell_kernel, mesh_shape),
        grid=(cells // width,),
        out_shape=[jax.ShapeDtypeStruct((2, slots), F32)] * 4
        + [jax.ShapeDtypeStruct((layers, cells), F32)] * 2,
        in_specs=[flat] * 2 + [firn] * 4 + [table] * 4,
        out_specs=[sums] * 4 + [firn] * 2,
        scratch_shapes=[
            pltpu.VMEM((chunks * WORDS * 8, LANES), jnp.int32),
            pltpu.VMEM((fields * 8, LANES), F32),
            pltpu.VMEM((LANES, 4 * chunks), F32),
        ]
        + [pltpu.VMEM((padded, LANES), F32)] * 12,
        compiler_params=kernel_params(VMEM_LARGE),
        name="cell_sums",
    )(position, weight, temp, water, density, limit, *tables)


def row_kernel(index, p0, p1, p2, p3, balance_out, albedo_out):
    blocks = balance_out.shape[0]
    per_place = index.shape[0] // 4
    one = jnp.ones((16, LANES), BF16)
    zero = jnp.zeros((16, LANES), BF16)
    lane_numbers = sixteens(LANES)
    block_numbers = sixteens(blocks)
    rights = []
    lefts = []
    for place, piece in enumerate((p0, p1, p2, p3)):
        for j in range(per_place):
            n = place * per_place + j
            row = index[n : n + 1, :]
            low_row = packed((row & (LANES - 1)).astype(F32))
            high_row = packed((row >> 7).astype(F32))
            rights.append(
                jnp.concatenate([jnp.where(low_row == m, one, zero) for m in lane_numbers], 0)
            )
            here = [high_row == m for m in block_numbers]
            parts = []
            for q in range(2):
                for term in two_terms(piece[q : q + 1, j * LANES : (j + 1) * LANES]):
                    value = packed(term)
                    parts += [jnp.where(h, value, zero) for h in here]
            lefts.append(jnp.concatenate(parts, 0))
    total = lax.dot_general(
        jnp.concatenate(lefts, 1),
        jnp.concatenate(rights, 1),
        (((1,), (1,)), ((), ())),
        preferred_element_type=F32,
    )
    balance_out[...] = total[:blocks] + total[blocks : 2 * blocks]
    albedo_out[...] = total[2 * blocks : 3 * blocks] + total[3 * blocks :]


def row_sums(index, pieces, rows):
    blocks = rows // LANES
    vmem = pl.BlockSpec(memory_space=pltpu.VMEM)
    return pl.pallas_call(
        row_kernel,
        out_shape=[jax.ShapeDtypeStruct((blocks, LANES), F32)] * 2,
        in_specs=[vmem] * 5,
        out_specs=[vmem] * 2,
        compiler_params=kernel_params(VMEM_SMALL),
        name="row_sums",
    )(index, *pieces)


def lay_flat(array):
    k, cells = array.shape
    return (
        array.reshape(k, cells // LANES, LANES).transpose(1, 0, 2).reshape(k * cells // LANES, LANES)
    )


def ring_partners(ice_count):
    even = [i ^ 1 for i in range(ice_count)]
    odd = [(((i - 1) ^ 1) + 1) % ice_count for i in range(ice_count)]
    return even, odd


def swap_partners(pieces, atm_count, ice_count):
    even, odd = ring_partners(ice_count)
    far = [(a, (a + atm_count // 2) % atm_count) for a in range(atm_count)]
    return [
        pieces[0],
        lax.ppermute(pieces[1], "ice", list(enumerate(even))),
        lax.ppermute(pieces[2], "ice", list(enumerate(odd))),
        lax.ppermute(pieces[3], "atm", far),
    ]


def on_device(driver, records, position, weight, temp, water, density, limit):
    fields, rows = driver.shape
    atm_count = lax.axis_size("atm")
    ice_count = lax.axis_size("ice")
    mesh_shape = (atm_count, ice_count)
    owners = atm_count * ice_count
    slots = records.shape[0] // owners
    records = records.reshape(owners, slots // LANES, LANES)
    *picked, index = pick_rows(mesh_shape, records, driver)
    tables = swap_partners(picked, atm_count, ice_count)
    *sums, temp_new, water_new = cell_sums(
        mesh_shape, lay_flat(position), lay_flat(weight), temp, water, density, limit, tables
    )
    returned = swap_partners(sums, atm_count, ice_count)
    balance, albedo = row_sums(index, returned, rows)
    return balance.reshape(rows), albedo.reshape(rows), temp_new, water_new


def solution(mesh):
    both = ("atm", "ice")
    return jax.shard_map(
        on_device,
        mesh=mesh,
        in_specs=(P(None, both), P(both)) + (P(None, both),) * 6,
        out_specs=(P(both), P(both), P(None, both), P(None, both)),
        check_vma=False,
    )
```

```python
import functools

import jax
import jax.numpy as jnp
from jax import lax
from jax.experimental import pallas as pl
from jax.experimental.pallas import tpu as pltpu
from jax.sharding import PartitionSpec as P

DIFFUSION_ITERS = 4
PERCOLATE_ROUNDS = 6
LANES = 128
TILE = 1024
F32 = jnp.float32
BF16 = jnp.bfloat16
WORDS = 5
FIXED = (1 << 20) - 1
VMEM_SMALL = 6 << 20
VMEM_MOST = 54950 << 10


def kernel_params(limit):
    return pltpu.CompilerParams(vmem_limit_bytes=limit)


def partner_ids(atm_count, ice_count):
    a = lax.axis_index("atm")
    i = lax.axis_index("ice")
    even = i ^ 1
    odd = lax.rem(((i + ice_count - 1) ^ 1) + 1, ice_count)
    far = lax.rem(a + atm_count // 2, atm_count)
    return (
        a * ice_count + i,
        a * ice_count + even,
        a * ice_count + odd,
        far * ice_count + i,
    )


def spread(row):
    return jnp.broadcast_to(row, (8, LANES))


def pick_kernel(mesh_shape, records, driver_any, o0, o1, o2, o3, index_out, driver, index, sems):
    ids = partner_ids(*mesh_shape)
    copies = [pltpu.make_async_copy(driver_any, driver, sems.at[4])]
    for place in range(4):
        copies.append(
            pltpu.make_async_copy(records.at[ids[place]], index.at[place], sems.at[place])
        )
    for copy in copies:
        copy.start()
    for copy in copies:
        copy.wait()
    fields, rows = driver.shape
    per_place = index.shape[1]
    for place, out in enumerate((o0, o1, o2, o3)):
        block = index[place]
        for j in range(per_place):
            row = block[j : j + 1, :]
            index_out[place * per_place + j : place * per_place + j + 1, :] = row
            where = spread(row)
            low = where & (LANES - 1)
            high = where >> 7
            total = jnp.zeros((fields, LANES), F32)
            for c in range(rows // LANES):
                found = jnp.take_along_axis(
                    driver[:, c * LANES : (c + 1) * LANES], low, axis=1
                )
                total = jnp.where(high == c, found, total)
            out[:, j * LANES : (j + 1) * LANES] = total


def pick_rows(mesh_shape, records, driver):
    fields = driver.shape[0]
    per_place = records.shape[1]
    slots = per_place * LANES
    vmem = pl.BlockSpec(memory_space=pltpu.VMEM)
    return pl.pallas_call(
        functools.partial(pick_kernel, mesh_shape),
        out_shape=[jax.ShapeDtypeStruct((fields, slots), F32)] * 4
        + [jax.ShapeDtypeStruct((4 * per_place, LANES), jnp.int32)],
        in_specs=[pl.BlockSpec(memory_space=pl.ANY)] * 2,
        out_specs=[vmem] * 5,
        scratch_shapes=[
            pltpu.VMEM(driver.shape, F32),
            pltpu.VMEM((4, per_place, LANES), jnp.int32),
            pltpu.SemaphoreType.DMA((5,)),
        ],
        compiler_params=kernel_params(VMEM_MOST),
        name="pick_rows",
    )(records, driver)


def to_layers(block, scratch, column, layers):
    for i in range(0, layers, 8):
        height = min(8, layers - i)
        for j in range(8):
            scratch[pl.ds(i * 8 + j * 8, height), :] = block[
                pl.ds(i, height), pl.ds(column + j * LANES, LANES)
            ]


def from_layers(block, scratch, column, layers):
    for i in range(0, layers, 8):
        height = min(8, layers - i)
        for j in range(8):
            block[pl.ds(i, height), pl.ds(column + j * LANES, LANES)] = scratch[
                pl.ds(i * 8 + j * 8, height), :
            ]


def layer(scratch, l):
    return scratch[pl.ds((l // 8) * 64 + l % 8, 8, stride=8), :]


def put_layer(scratch, l, value):
    scratch[pl.ds((l // 8) * 64 + l % 8, 8, stride=8), :] = value


class Conduct:
    def __init__(self, low, layers):
        self.low = low
        self.layers = layers
        self.temps = [dict() for _ in range(DIFFUSION_ITERS + 1)]
        self.flows = [dict() for _ in range(DIFFUSION_ITERS + 1)]
        self.between = {}
        self.conductance = {}

    def add(self, l, temp, density):
        self.temps[0][l] = temp
        self.conductance[l] = 0.2 + 0.25 * density
        if l > self.low:
            self.between[l - 1] = 0.5 * (self.conductance[l] + self.conductance[l - 1])
        for s in range(1, DIFFUSION_ITERS + 1):
            self.sweep(s, l - s)
        if l == self.layers - 1:
            for extra in range(1, DIFFUSION_ITERS + 1):
                for s in range(1, DIFFUSION_ITERS + 1):
                    self.sweep(s, l + extra - s)

    def sweep(self, s, m):
        before = self.temps[s - 1]
        bottom = m == self.layers - 1
        if m in self.temps[s] or m not in before:
            return
        if not bottom:
            if m + 1 not in before or m not in self.between:
                return
            self.flows[s][m] = self.between[m] * (before[m + 1] - before[m])
        if m > 0 and (m - 1) not in self.flows[s]:
            return
        value = before[m]
        if not bottom:
            value = value + self.flows[s][m]
        if m > 0:
            value = value - self.flows[s][m - 1]
        self.temps[s][m] = value


class Column:
    def __init__(self, temp, water, limit, half=None):
        self.half = -0.5 * temp if half is None else half
        self.water = water
        self.limit = limit
        self.leaving = {}

    def leave(self, r):
        held = jnp.minimum(self.water, self.limit)
        self.leaving[r] = self.water - held
        return held

    def round(self, r, arriving):
        held = self.leave(r)
        if arriving is not None:
            held = held + arriving
        frozen = jnp.minimum(held, jnp.maximum(self.half, 0.0))
        self.water = held - frozen
        self.half = self.half - 0.75 * frozen


def open_layers():
    return range(DIFFUSION_ITERS + 1, DIFFUSION_ITERS + PERCOLATE_ROUNDS)


def deep_steps(st, sw, sd, sl, ot, ow, layers, found):
    reach = DIFFUSION_ITERS
    conduct = Conduct(1, layers)
    columns = {}
    ready = reach
    for l in range(1, layers):
        conduct.add(l, layer(st, l), layer(sd, l))
        yield
        while ready < layers and (ready == reach or ready in conduct.temps[reach]):
            m = ready
            ready += 1
            if m == reach:
                columns[m] = Column(jnp.zeros((8, LANES), F32), layer(sw, m), layer(sl, m))
                columns[m].leave(0)
                continue
            column = Column(conduct.temps[reach][m], layer(sw, m), layer(sl, m))
            columns[m] = column
            rounds = min(m - reach, PERCOLATE_ROUNDS)
            for r in range(rounds):
                column.round(r, columns[m - 1].leaving[r])
                yield
            if rounds < PERCOLATE_ROUNDS:
                column.leave(rounds)
            else:
                put_layer(ot, m, -2.0 * column.half)
                put_layer(ow, m, column.water)
            if m - 1 >= reach + PERCOLATE_ROUNDS:
                del columns[m - 1]
            yield
    last = columns[layers - 1].leaving
    runoff = last[0]
    for r in range(1, PERCOLATE_ROUNDS):
        runoff = runoff + last[r]
    found["runoff"] = runoff
    found["columns"] = columns


def upper_steps(st, sw, sd, sl, ot, ow, top, gain, columns):
    reach = DIFFUSION_ITERS
    conduct = Conduct(0, 1 << 20)
    above = None
    for l in range(2 * reach + 1):
        conduct.add(l, top if l == 0 else layer(st, l), layer(sd, l))
        yield
        m = l - reach
        if m < 0:
            continue
        water = layer(sw, m)
        if m == 0:
            water = water + gain
        column = Column(conduct.temps[reach][m], water, layer(sl, m))
        for r in range(PERCOLATE_ROUNDS):
            column.round(r, None if above is None else above.leaving[r])
            yield
        put_layer(ot, m, -2.0 * column.half)
        put_layer(ow, m, column.water)
        above = column
    for m in range(reach + 1, reach + PERCOLATE_ROUNDS):
        column = columns[m]
        for r in range(m - reach, PERCOLATE_ROUNDS):
            column.round(r, above.leaving[r])
            yield
        put_layer(ot, m, -2.0 * column.half)
        put_layer(ow, m, column.water)
        above = column


def together(*lines):
    ticks = 64
    for tick in range(1, ticks + 1):
        for steps, length in lines:
            for _ in range(length * tick // ticks - length * (tick - 1) // ticks):
                next(steps, None)
    for steps, _ in lines:
        for _ in steps:
            pass


def two_terms(value):
    first = value.astype(BF16).astype(F32)
    return first, value - first


def make_words(rows, scale):
    q = (rows * scale + 0.5).astype(jnp.int32)
    q = [spread(q[f : f + 1, :]) for f in range(8)]
    return [
        q[0] | ((q[5] & 0xFFF) << 20),
        q[1] | ((q[5] >> 12) << 20) | ((q[6] & 0xF) << 28),
        q[2] | (((q[6] >> 4) & 0xFFF) << 20),
        q[3] | ((q[6] >> 16) << 20) | ((q[7] & 0xFF) << 24),
        q[4] | ((q[7] >> 8) << 20),
    ]


def from_words(words):
    def high(word, bits):
        return lax.shift_right_logical(word, jnp.full(word.shape, bits, jnp.int32))

    q = [word & FIXED for word in words]
    q.append(high(words[0], 20) | ((high(words[1], 20) & 0xFF) << 12))
    q.append(
        high(words[1], 28) | (high(words[2], 20) << 4) | ((high(words[3], 20) & 0xF) << 16)
    )
    q.append(high(words[3], 24) | (high(words[4], 20) << 8))
    return [value.astype(F32) for value in q]


def gather_steps(table, low, high, weights, chunks, forced):
    for k in range(len(low)):
        found = [jnp.zeros((8, LANES), jnp.int32) for _ in range(WORDS)]
        for c in range(chunks):
            here = high[k] == c
            for n in range(WORDS):
                value = jnp.take_along_axis(
                    table[pl.ds((c * WORDS + n) * 8, 8), :], low[k], axis=1
                )
                found[n] = jnp.where(here, value, found[n])
            yield
        for f, value in enumerate(from_words(found)):
            part = value * weights[k]
            forced[f] = part if k == 0 else forced[f] + part


def packed(row):
    return jnp.broadcast_to(row, (16, LANES)).astype(BF16)


def sixteens(count):
    base = lax.broadcasted_iota(jnp.int32, (16, LANES), 0)
    return [(base + 16 * j).astype(F32).astype(BF16) for j in range(count // 16)]


def scatter_steps(total, low, high, weights, values, chunks):
    one = jnp.ones((16, LANES), BF16)
    zero = jnp.zeros((16, LANES), BF16)
    lane_numbers = sixteens(LANES)
    chunk_numbers = sixteens(chunks)
    for k in range(len(low)):
        terms = [t for v in values for t in two_terms(v * weights[k])]
        low_f = low[k].astype(F32)
        high_f = high[k].astype(F32)
        lefts = []
        rights = []
        for s in range(8):
            low_row = packed(low_f[s : s + 1, :])
            high_row = packed(high_f[s : s + 1, :])
            rights.append(
                jnp.concatenate([jnp.where(low_row == n, one, zero) for n in lane_numbers], 0)
            )
            here = [high_row == n for n in chunk_numbers]
            parts = []
            for term in terms:
                row = packed(term[s : s + 1, :])
                parts += [jnp.where(h, row, zero) for h in here]
            lefts.append(jnp.concatenate(parts, 0))
            yield
        total[...] += lax.dot_general(
            jnp.concatenate(rights, 1),
            jnp.concatenate(lefts, 1),
            (((1,), (1,)), ((), ())),
            preferred_element_type=F32,
        )


def tile_groups(tiles):
    return (0, 1, 5, tiles)


def cell_kernel(mesh_shape, *refs):
    afar = refs[:6]
    t0, t1, t2, t3 = refs[6:10]
    o0, o1, o2, o3 = refs[10:14]
    table, units, total = refs[16:19]
    laid = (refs[19:25], refs[25:31])
    near = refs[31:37]
    position, weight, temp, water, density, limit = near
    results = refs[37:39]
    temp_out, water_out = results
    in_sems, out_sems = refs[39:41]
    tiles = temp.shape[1] // TILE
    bounds = tile_groups(tiles)
    groups = len(bounds) - 1

    def arrivals(group):
        tile, count = bounds[group], bounds[group + 1] - bounds[group]
        copies = []
        for n in range(6):
            if n < 2:
                part = (pl.ds(pl.multiple_of(tile * 32, 32), count * 32), slice(None))
            else:
                part = (slice(None), pl.ds(pl.multiple_of(tile * TILE, TILE), count * TILE))
            copies.append(
                pltpu.make_async_copy(afar[n].at[part], near[n].at[part], in_sems.at[group, n])
            )
        return copies

    def departures(group):
        part = (slice(None), pl.ds(pl.multiple_of(group * 2 * TILE, TILE), 2 * TILE))
        return [
            pltpu.make_async_copy(results[n].at[part], refs[14 + n].at[part], out_sems.at[group, n])
            for n in range(2)
        ]

    for group in range(groups):
        for copy in arrivals(group):
            copy.start()
    fields, slots = t0.shape
    per_place = slots // LANES
    chunks = 4 * per_place
    layers, width = temp.shape
    ids = partner_ids(*mesh_shape)

    rows = [
        (t0, t1, t2, t3)[c // per_place][
            :, (c % per_place) * LANES : (c % per_place + 1) * LANES
        ]
        for c in range(chunks)
    ]
    most = rows[0]
    for row in rows[1:]:
        most = jnp.maximum(most, row)
    most = jnp.broadcast_to(jnp.max(most, axis=1, keepdims=True), (fields, LANES))
    most = jnp.maximum(most, 1e-30)
    scale = float(FIXED) / most
    for f in range(fields):
        units[pl.ds(f * 8, 8), :] = spread(most[f : f + 1, :] * (1.0 / FIXED))
    for c in range(chunks):
        for n, word in enumerate(make_words(rows[c], scale)):
            table[pl.ds((c * WORDS + n) * 8, 8), :] = word
    total[...] = jnp.zeros(total.shape, F32)

    def columns_of(tile):
        return pl.multiple_of(tile * TILE, TILE)

    def lines_before(tile, parity, state):
        st, sw, sd, sl, ot, ow = laid[parity]
        column = columns_of(tile)
        low = []
        high = []
        weights = []
        for k in range(4):
            rows = pl.ds(tile * 32 + k, 8, stride=4)
            p = position[rows, :]
            owner = p >> (slots.bit_length() - 1)
            place = jnp.zeros((8, LANES), jnp.int32)
            for n in range(1, 4):
                place = jnp.where(owner == ids[n], n, place)
            low.append(p & (LANES - 1))
            high.append(place * per_place + ((p & (slots - 1)) >> 7))
            weights.append(weight[rows, :])
        to_layers(temp, st, column, layers)
        to_layers(density, sd, column, layers)
        to_layers(water, sw, column, layers)
        to_layers(limit, sl, column, layers)
        state.update(low=low, high=high, weights=weights, forced=[None] * fields)
        return [
            (gather_steps(table, low, high, weights, chunks, state["forced"]), 64),
            (deep_steps(*laid[parity], layers, state), 230),
        ]

    def surface(parity, state):
        forced = [value * units[pl.ds(f * 8, 8), :] for f, value in enumerate(state["forced"])]
        air = 2.0 * forced[0] - 1.0
        short, long, snow, rain, humid, wind, press = forced[1:]
        albedo = 0.45 + 0.4 * snow / (snow + 0.1) - 0.1 * jnp.maximum(air, 0.0)
        skin = layer(laid[parity][0], 0)
        flux = (
            1.5 * (1.0 - albedo) * short
            + 0.6 * (long - 0.5)
            + 0.5 * wind * (air - skin)
            + 0.3 * wind * (humid - press)
        )
        top = skin + 0.5 * flux
        balance = snow + rain - state["runoff"] - 0.2 * wind * (press - humid)
        parts = [balance, albedo, jnp.minimum(top, 0.0), jnp.maximum(top, 0.0) + rain]
        for m in open_layers():
            parts += [state["columns"][m].half, state["columns"][m].water]
        return tuple(parts + state["low"] + state["high"] + state["weights"])

    def lines_after(parity, carry):
        st, sw, sd, sl, ot, ow = laid[parity]
        balance, albedo, top, gain = carry[:4]
        columns = {}
        for n, m in enumerate(open_layers()):
            columns[m] = Column(None, carry[5 + 2 * n], layer(sl, m), carry[4 + 2 * n])
        low, high, weights = carry[-12:-8], carry[-8:-4], carry[-4:]
        return [
            (scatter_steps(total, low, high, weights, (balance, albedo), chunks), 32),
            (upper_steps(*laid[parity], top, gain, columns), 54),
        ]

    def write(tile, parity):
        from_layers(temp_out, laid[parity][4], columns_of(tile), layers)
        from_layers(water_out, laid[parity][5], columns_of(tile), layers)

    def advance(tile, parity, carry):
        state = {}
        lines = lines_after(parity, carry) + lines_before(tile + 1, 1 - parity, state)
        together(*lines)
        write(tile, parity)
        return surface(1 - parity, state)

    for copy in arrivals(0):
        copy.wait()
    state = {}
    together(*lines_before(0, 0, state))
    carry = surface(0, state)
    def two_tiles(i, carry):
        carry = advance(2 * i, 0, carry)
        carry = advance(2 * i + 1, 1, carry)
        for copy in departures(i):
            copy.start()
        return carry

    for group in range(1, groups):
        for copy in arrivals(group):
            copy.wait()
        first, last = bounds[group] // 2, (bounds[group + 1] - 1) // 2
        carry = lax.fori_loop(first, last, two_tiles, carry)
    carry = advance(tiles - 2, 0, carry)
    together(*lines_after(1, carry))
    write(tiles - 1, 1)
    for copy in departures(tiles // 2 - 1):
        copy.start()

    sums = total[...].T
    for q in range(2):
        first = sums[2 * q * chunks : (2 * q + 1) * chunks]
        second = sums[(2 * q + 1) * chunks : (2 * q + 2) * chunks]
        both = first + second
        for c in range(chunks):
            j = c % per_place
            (o0, o1, o2, o3)[c // per_place][q : q + 1, j * LANES : (j + 1) * LANES] = both[
                c : c + 1, :
            ]

    for group in range(tiles // 2):
        for copy in departures(group):
            copy.wait()


def cell_sums(mesh_shape, position, weight, temp, water, density, limit, tables):
    fields, slots = tables[0].shape
    chunks = 4 * slots // LANES
    layers, cells = temp.shape
    vmem = pl.BlockSpec(memory_space=pltpu.VMEM)
    anywhere = pl.BlockSpec(memory_space=pl.ANY)
    tiles = cells // TILE
    padded = -(-layers // 8) * 64
    return pl.pallas_call(
        functools.partial(cell_kernel, mesh_shape),
        out_shape=[jax.ShapeDtypeStruct((2, slots), F32)] * 4
        + [jax.ShapeDtypeStruct((layers, cells), F32)] * 2,
        in_specs=[anywhere] * 6 + [vmem] * 4,
        out_specs=[vmem] * 4 + [anywhere] * 2,
        scratch_shapes=[
            pltpu.VMEM((chunks * WORDS * 8, LANES), jnp.int32),
            pltpu.VMEM((fields * 8, LANES), F32),
            pltpu.VMEM((LANES, 4 * chunks), F32),
        ]
        + [pltpu.VMEM((padded, LANES), F32)] * 12
        + [pltpu.VMEM(position.shape, jnp.int32), pltpu.VMEM(weight.shape, F32)]
        + [pltpu.VMEM((layers, cells), F32)] * 6
        + [pltpu.SemaphoreType.DMA((3, 6)), pltpu.SemaphoreType.DMA((tiles // 2, 2))],
        compiler_params=kernel_params(VMEM_MOST),
        name="cell_sums",
    )(position, weight, temp, water, density, limit, *tables)


def row_kernel(index, p0, p1, p2, p3, balance_out, albedo_out):
    blocks = balance_out.shape[0]
    per_place = index.shape[0] // 4
    one = jnp.ones((16, LANES), BF16)
    zero = jnp.zeros((16, LANES), BF16)
    lane_numbers = sixteens(LANES)
    block_numbers = sixteens(blocks)
    rights = []
    lefts = []
    for place, piece in enumerate((p0, p1, p2, p3)):
        for j in range(per_place):
            n = place * per_place + j
            row = index[n : n + 1, :]
            low_row = packed((row & (LANES - 1)).astype(F32))
            high_row = packed((row >> 7).astype(F32))
            rights.append(
                jnp.concatenate([jnp.where(low_row == m, one, zero) for m in lane_numbers], 0)
            )
            here = [high_row == m for m in block_numbers]
            parts = []
            for q in range(2):
                for term in two_terms(piece[q : q + 1, j * LANES : (j + 1) * LANES]):
                    value = packed(term)
                    parts += [jnp.where(h, value, zero) for h in here]
            lefts.append(jnp.concatenate(parts, 0))
    total = lax.dot_general(
        jnp.concatenate(lefts, 1),
        jnp.concatenate(rights, 1),
        (((1,), (1,)), ((), ())),
        preferred_element_type=F32,
    )
    balance_out[...] = total[:blocks] + total[blocks : 2 * blocks]
    albedo_out[...] = total[2 * blocks : 3 * blocks] + total[3 * blocks :]


def row_sums(index, pieces, rows):
    blocks = rows // LANES
    vmem = pl.BlockSpec(memory_space=pltpu.VMEM)
    return pl.pallas_call(
        row_kernel,
        out_shape=[jax.ShapeDtypeStruct((blocks, LANES), F32)] * 2,
        in_specs=[vmem] * 5,
        out_specs=[vmem] * 2,
        compiler_params=kernel_params(VMEM_SMALL),
        name="row_sums",
    )(index, *pieces)


def lay_flat(array):
    k, cells = array.shape
    return (
        array.reshape(k, cells // LANES, LANES).transpose(1, 0, 2).reshape(k * cells // LANES, LANES)
    )


def ring_partners(ice_count):
    even = [i ^ 1 for i in range(ice_count)]
    odd = [(((i - 1) ^ 1) + 1) % ice_count for i in range(ice_count)]
    return even, odd


def swap_partners(pieces, atm_count, ice_count):
    even, odd = ring_partners(ice_count)
    far = [(a, (a + atm_count // 2) % atm_count) for a in range(atm_count)]
    return [
        pieces[0],
        lax.ppermute(pieces[1], "ice", list(enumerate(even))),
        lax.ppermute(pieces[2], "ice", list(enumerate(odd))),
        lax.ppermute(pieces[3], "atm", far),
    ]


def on_device(driver, records, position, weight, temp, water, density, limit):
    fields, rows = driver.shape
    atm_count = lax.axis_size("atm")
    ice_count = lax.axis_size("ice")
    mesh_shape = (atm_count, ice_count)
    owners = atm_count * ice_count
    slots = records.shape[0] // owners
    records = records.reshape(owners, slots // LANES, LANES)
    *picked, index = pick_rows(mesh_shape, records, driver)
    tables = swap_partners(picked, atm_count, ice_count)
    *sums, temp_new, water_new = cell_sums(
        mesh_shape, lay_flat(position), lay_flat(weight), temp, water, density, limit, tables
    )
    returned = swap_partners(sums, atm_count, ice_count)
    balance, albedo = row_sums(index, returned, rows)
    return balance.reshape(rows), albedo.reshape(rows), temp_new, water_new


def solution(mesh):
    both = ("atm", "ice")
    return jax.shard_map(
        on_device,
        mesh=mesh,
        in_specs=(P(None, both), P(both)) + (P(None, both),) * 6,
        out_specs=(P(both), P(both), P(None, both), P(None, both)),
        check_vma=False,
    )
```
